768 devices in a mesh: img: 96 (over x, y, z_lo), txt: 8 (over z_hi, core).
Axes of the slice: x: 4, y: 8, z: 12 (z_hi: 4, z_lo: 3; z = z_hi * 3 + z_lo), core: 2. Of those that a mesh axis runs over, the one named last changes fastest.
Arguments:
- image_emb: float32 [12288, 768], P(('img', 'txt')), may hold values from -0.6 to 0.6
- text_emb: float32 [12288, 768], P(('txt', 'img')), may hold values from -0.6 to 0.6
- pairs: int32 [12288], P('img'), may hold values from 0 to 12287, each once
- log_scale: float32 [1], replicated, may hold values from 2 to 2.6
- bias: float32 [1], replicated, may hold values from -12 to -8
Outputs:
- image_loss: float32 [12288], P('img')
- image_grad: float32 [12288, 768], P(('img', 'txt'))
- text_grad: float32 [12288, 768], P(('txt', 'img'))
The draws below stay inside these ranges and needn't reach their ends.
Inputs may be any that keep to these rules, and one draw needn't show every extreme that they name: `pairs`: each text is matched to exactly one image.
All inputs are finite; a program needn't handle non-finite values.
Results may differ from the reference program's by a relative error of at most 0.0003.
Values sent between devices are 32-bit elements; how exact they have to be, the bound alone decides.
A program may use at most 32 MiB of HBM per device.

```python
import jax
import jax.numpy as jnp
from jax import lax

E = 768
NI = 12288
NT = 12288
N_IMG = 96


def block_levels(key, shape, shards, low, high):
    level, own = 1.0, jax.random.fold_in(key, 6)
    for axis_at, blocks in shards:
        steps = jnp.exp(jax.random.uniform(jax.random.fold_in(own, axis_at), (blocks,), jnp.float32, low / len(shards), high / len(shards)))
        level = level * jnp.repeat(steps, shape[axis_at] // blocks).reshape([-1 if axis == axis_at else 1 for axis in range(len(shape))])
    return level


def noise(own_key, shape, scale, reach, cuts=(), kind=jnp.bfloat16):
    array = scale * jax.random.normal(own_key, shape, jnp.float32)
    if cuts:
        array = array * block_levels(own_key, shape, cuts, -0.22, 0.18)
    return jnp.clip(array, -reach, reach).astype(kind)


def setup_inputs(seed: int = 0) -> dict:
    key_of = jax.random.split(jax.random.key(seed), 6)
    image_emb = noise(key_of[0], (NI, E), 0.104, 0.6, ((0, 768),), jnp.float32)
    text_emb = noise(key_of[1], (NT, E), 0.104, 0.6, ((0, 768),), jnp.float32)
    pairs = jax.random.permutation(key_of[2], NT).astype(jnp.int32)
    log_scale = jnp.clip(jax.random.uniform(key_of[3], (1,), jnp.float32, 2.0, 2.6), 2.0, 2.6)
    bias = jnp.clip(jax.random.uniform(key_of[4], (1,), jnp.float32, -12.0, -8.0), -12.0, -8.0)
    return {"image_emb": image_emb, "text_emb": text_emb, "pairs": pairs, "log_scale": log_scale, "bias": bias}


def reference(image_emb, text_emb, pairs, log_scale, bias):
    scale = jnp.exp(log_scale[0])
    shift = bias[0]
    rows = image_emb.shape[0]
    nblk = max(N_IMG // 8, 1)
    block = rows // nblk
    width = image_emb.shape[1]
    img_blocks = image_emb.reshape(nblk, block, width)
    pair_blocks = pairs.reshape(nblk, block)
    columns = jnp.arange(text_emb.shape[0], dtype=jnp.int32)

    def step(total, item):
        images, matched = item
        dots = lax.dot_general(images, text_emb, (((1,), (1,)), ((), ())), precision=lax.Precision.HIGHEST, preferred_element_type=jnp.float32)
        logits = scale * dots + shift
        sign = jnp.where(matched[:, None] == columns[None, :], 1.0, -1.0).astype(logits.dtype)
        loss = jnp.sum(jax.nn.softplus(-sign * logits), axis=1)
        dlogits = -sign * jax.nn.sigmoid(-sign * logits)
        grad_img = scale * jnp.dot(dlogits, text_emb, precision=lax.Precision.HIGHEST, preferred_element_type=jnp.float32)
        grad_txt = lax.dot_general(dlogits, images, (((0,), (0,)), ((), ())), precision=lax.Precision.HIGHEST, preferred_element_type=jnp.float32)
        return total + scale * grad_txt, (loss, grad_img)

    text_grad, (losses, grads) = lax.scan(step, jnp.zeros_like(text_emb), (img_blocks, pair_blocks))
    return losses.reshape(rows), grads.reshape(rows, width), text_grad
```

```python
import functools

import jax
import jax.numpy as jnp
from jax import lax
from jax.experimental import pallas as pl
from jax.experimental.pallas import tpu as pltpu
from jax.sharding import PartitionSpec as P

MESH = pl.DeviceIdType.MESH
NX, NY, NZ, ZLO = 4, 8, 12, 3
ROWS, WIDTH = 16, 768
CA = 256
CB = WIDTH - CA
TEXTS = 2 * NZ * ROWS
F32, BF16 = jnp.float32, jnp.bfloat16
COPIES = 128
STEP = (0, 1, -1)


def halves(value):
    high = value.astype(BF16)
    return high, (value - high.astype(F32)).astype(BF16)


def dot3(ah, al, bh, bl, dims):
    def dot(a, b):
        return lax.dot_general(a, b, (dims, ((), ())), preferred_element_type=F32)

    return dot(ah, bh) + (dot(ah, bl) + dot(al, bh))


def kernel(
    log_scale_ref, bias_ref, pairs_ref, image_ref, text_ref,
    loss_ref, image_grad_ref, text_grad_ref,
    ga, gb, tx, xh, xl, th, tl, dh, dl, pc,
    xga, xgb, tg, rxb, rya, ryb, rxa, rc, rz, rk, py, px, ly, lx, lz,
    local_sem, send_sem, recv_sem,
):
    img, txt = lax.axis_index("img"), lax.axis_index("txt")
    column = lax.div(img, ZLO)
    x, y = lax.div(column, NY), lax.rem(column, NY)
    core = lax.rem(txt, 2)
    z = lax.div(txt, 2) * ZLO + lax.rem(img, ZLO)
    way = 1 - 2 * core

    def moved(at, by, size):
        return lax.rem(at + way * by + 2 * size, size)

    def device(at_x, at_y, at_z, at_core):
        return (
            (at_x * NY + at_y) * ZLO + lax.rem(at_z, ZLO),
            lax.div(at_z, ZLO) * 2 + at_core,
        )

    def along_x(by):
        return device(moved(x, by, NX), y, z, core)

    def along_y(by):
        return device(x, moved(y, by, NY), z, core)

    def along_z(by):
        return device(x, y, moved(z, by, NZ), core)

    sibling = device(x, y, z, 1 - core)
    peers = [along_x(by) for by in (1, -1, 2)]
    peers += [along_y(by) for by in (1, -1, 2, -2)]
    peers += [along_z(by) for by in (1, -1, 3, -3, 6)]
    peers.append(sibling)

    copies = [
        pltpu.make_async_copy(image_ref.at[:, pl.ds(0, CA)], ga.at[0, 0], local_sem.at[0]),
        pltpu.make_async_copy(image_ref.at[:, pl.ds(CA, CB)], gb.at[0, 0], local_sem.at[1]),
        pltpu.make_async_copy(text_ref, tx.at[0, 0, 0], local_sem.at[2]),
    ]
    for copy in copies:
        copy.start()

    barrier = pltpu.get_barrier_semaphore()
    for peer in peers:
        pl.semaphore_signal(barrier, inc=1, device_id=peer, device_id_type=MESH)

    lane = lax.broadcasted_iota(jnp.int32, (8, 128), 1)
    row = lax.broadcasted_iota(jnp.int32, (8, 128), 0)
    own = 2 * (x * NY + y)
    pairs_row = jnp.broadcast_to(pairs_ref[...].astype(F32), (8, 128))
    tile = jnp.zeros((8, 128), F32)
    for half in range(2):
        picked = jnp.where(lane == txt * ROWS + half * 8 + row, pairs_row, 0.0)
        tile = jnp.where(lane == own + half, jnp.sum(picked, axis=1, keepdims=True), tile)
    py[0] = tile

    pl.semaphore_wait(barrier, len(peers))
    for copy in copies:
        copy.wait()

    started = []

    def send(source, target, to):
        at = len(started)
        copy = pltpu.make_async_remote_copy(
            src_ref=source,
            dst_ref=target,
            send_sem=send_sem.at[at],
            recv_sem=recv_sem.at[at],
            device_id=to,
            device_id_type=MESH,
        )
        copy.start()
        started.append(copy)
        return copy

    def arrived(*copies):
        for copy in copies:
            copy.wait_recv()

    a_x = [send(ga.at[0, 0], ga.at[0, by % NX], along_x(by)) for by in (2, 1, -1)]
    b_y2 = [send(gb.at[0, 0], gb.at[0, by % NY], along_y(by)) for by in (2, -2)]
    t6 = send(tx.at[0, 0, 0], tx.at[0, 0, 2], along_z(6))
    t3 = [send(tx.at[0, 0, 0], tx.at[0, 0, k], along_z(by)) for k, by in ((1, 3), (3, -3))]
    b_y1 = [send(gb.at[0, 0], gb.at[0, by % NY], along_y(by)) for by in (1, -1)]
    p_y2 = [send(py.at[0], py.at[by % NY], along_y(by)) for by in (2, -2)]
    p_y1 = [send(py.at[0], py.at[by % NY], along_y(by)) for by in (1, -1)]
    t_near = [send(tx.at[0, 0, 0], tx.at[0, e, 0], along_z(STEP[e])) for e in (1, 2)]
    b_x = [send(gb.at[0, 0], gb.at[by % NX, 0], along_x(by)) for by in (2, 1, -1)]

    arrived(*a_x)
    a_y2 = [send(ga.at[0], ga.at[by % NY], along_y(by)) for by in (2, -2)]
    arrived(*b_y2)
    b_far = [
        send(gb.at[0, 2], gb.at[0, 4], along_y(2)),
        send(gb.at[0, 2], gb.at[0, 3], along_y(1)),
        send(gb.at[0, 6], gb.at[0, 5], along_y(-1)),
    ]
    a_y1 = [send(ga.at[0], ga.at[by % NY], along_y(by)) for by in (1, -1)]
    arrived(*b_y1)
    for low in (1, 6):
        b_x += [
            send(gb.at[0, pl.ds(low, 2)], gb.at[by % NX, pl.ds(low, 2)], along_x(by))
            for by in (2, 1, -1)
        ]
    arrived(*p_y2)
    p_far = [
        send(py.at[2], py.at[4], along_y(2)),
        send(py.at[2], py.at[3], along_y(1)),
        send(py.at[6], py.at[5], along_y(-1)),
    ]
    arrived(*t3)
    for k in (1, 3):
        t_near += [send(tx.at[0, 0, k], tx.at[0, e, k], along_z(STEP[e])) for e in (1, 2)]
    arrived(*a_y2)
    a_far = [
        send(ga.at[2], ga.at[4], along_y(2)),
        send(ga.at[2], ga.at[3], along_y(1)),
        send(ga.at[6], ga.at[5], along_y(-1)),
    ]
    arrived(*b_far)
    b_x += [
        send(gb.at[0, pl.ds(3, 3)], gb.at[by % NX, pl.ds(3, 3)], along_x(by))
        for by in (2, 1, -1)
    ]
    arrived(t6)
    t_near += [send(tx.at[0, 0, 2], tx.at[0, e, 2], along_z(STEP[e])) for e in (1, 2)]
    t_core = [send(tx.at[0, 0], tx.at[1, 0], sibling)]
    arrived(*p_y1, *p_far)
    px[0] = jnp.sum(py[...], axis=0)
    p_x = [send(px.at[0], px.at[by % NX], along_x(by)) for by in (2, 1, -1)]

    places = lax.broadcasted_iota(jnp.int32, (8, TEXTS), 1)
    slot = lax.div(places, ROWS)
    ids = places
    for s in range(2):
        for e in range(3):
            for k in range(4):
                at = (s * 3 + e) * 4 + k
                by = 3 * k + STEP[e]
                at_z = moved(z, by if s else -by, NZ)
                at_core = 1 - core if s else core
                owner = lax.div(at_z, ZLO) * 2 + at_core
                base = owner * (NX * NY * ZLO * ROWS) + (column * ZLO + lax.rem(at_z, ZLO)) * ROWS
                ids = jnp.where(slot == at, places + (base - at * ROWS), ids)
    ids = ids.astype(F32)[0:1]

    arrived(*t_near)
    t_core.append(send(tx.at[0, pl.ds(1, 2)], tx.at[1, pl.ds(1, 2)], sibling))

    arrived(*p_x)
    matched = jnp.sum(px[...], axis=0)

    def lane_of(ox, oy, half):
        return 2 * (moved(x, -ox, NX) * NY + moved(y, -oy, NY)) + half

    for ox in range(NX):
        for oy in range(NY):
            for half in range(2):
                picked = jnp.where(lane == lane_of(ox, oy, half), matched, 0.0)
                spread = jnp.broadcast_to(jnp.sum(picked, axis=1, keepdims=True), (8, 128))
                pc[pl.ds(((ox * NY + oy) * 2 + half) * 8, 8), :] = spread

    arrived(*t_core)
    for s in range(2):
        high, low = halves(tx[s].reshape(NZ * ROWS, WIDTH))
        th[pl.ds(s * NZ * ROWS, NZ * ROWS), :] = high
        tl[pl.ds(s * NZ * ROWS, NZ * ROWS), :] = low
    arrived(*a_y1, *a_far)
    for ox in range(NX):
        high, low = halves(ga[:, ox].reshape(NY * ROWS, CA))
        xh[pl.ds(ox * NY * ROWS, NY * ROWS), pl.ds(0, CA)] = high
        xl[pl.ds(ox * NY * ROWS, NY * ROWS), pl.ds(0, CA)] = low
    arrived(*b_x)
    for ox in range(NX):
        high, low = halves(gb[ox].reshape(NY * ROWS, CB))
        xh[pl.ds(ox * NY * ROWS, NY * ROWS), pl.ds(CA, CB)] = high
        xl[pl.ds(ox * NY * ROWS, NY * ROWS), pl.ds(CA, CB)] = low

    scale = jnp.exp(jnp.full((8, 128), log_scale_ref[0], F32))[0:1, 0:1]
    shift = bias_ref[0]
    losses = jnp.zeros((8, 128), F32)
    r_x = []
    for ox in (2, 1, 3, 0):
        rows = pl.ds(ox * NY * ROWS, NY * ROWS)
        dots = dot3(xh[rows, :], xl[rows, :], th[...], tl[...], ((1,), (1,)))
        logits = scale * dots + shift
        pair = pc[rows, :]
        match = jnp.concatenate([pair] * (TEXTS // 128), axis=1) == ids
        signed = jnp.where(match, -logits, logits)
        small = jnp.exp(-jnp.abs(logits))
        loss = jnp.maximum(signed, 0.0) + jnp.log1p(small)
        loss = sum(loss[:, at * 128 : (at + 1) * 128] for at in range(TEXTS // 128))
        loss = jnp.sum(loss, axis=1, keepdims=True)
        for oy in range(NY):
            for half in range(2):
                at = (oy * 2 + half) * 8
                losses = jnp.where(lane == lane_of(ox, oy, half), loss[at : at + 8], losses)
        part = 1.0 / (1.0 + small)
        chance = jnp.where(signed >= 0.0, part, small * part)
        slope = scale * jnp.where(match, -chance, chance)
        high, low = halves(slope)
        dh[rows, :] = high
        dl[rows, :] = low
        grad = dot3(high, low, th[...], tl[...], ((1,), (0,)))
        xgb[ox] = grad[:, CA:].reshape(NY, ROWS, CB)
        for oy in range(NY):
            xga[oy, ox] = grad[oy * ROWS : (oy + 1) * ROWS, :CA]
        if ox:
            r_x.append(send(xgb.at[ox], rxb.at[ox - 1], along_x(-ox)))
    ly[0] = losses
    l_y2 = [send(ly.at[0], ly.at[by % NY], along_y(by)) for by in (2, -2)]
    l_y1 = [send(ly.at[0], ly.at[by % NY], along_y(by)) for by in (1, -1)]

    def y_first(source, target):
        far = [
            send(source(4), target(4), along_y(-2)),
            send(source(3), target(3), along_y(-1)),
            send(source(5), target(5), along_y(1)),
        ]
        near = [send(source(1), target(1), along_y(-1)), send(source(7), target(7), along_y(1))]
        return far, near

    def y_second(source, target, far):
        arrived(*far)
        source(2)[...] += target(3)[...] + target(4)[...]
        source(6)[...] += target(5)[...]
        return [send(source(2), target(2), along_y(-2)), send(source(6), target(6), along_y(2))]

    a_far, a_near = y_first(lambda o: xga.at[o], lambda o: rya.at[o])

    def text_part(at):
        cols = pl.ds(at * 128, 128)
        part = dot3(dh[:, cols], dl[:, cols], xh[...], xl[...], ((0,), (0,)))
        part = part.reshape(8, ROWS, WIDTH)
        for i in range(8):
            s, rest = divmod(at * 8 + i, 12)
            e, k = divmod(rest, 4)
            tg[s, e, k] = part[i]

    text_part(2)
    text_part(1)
    r_core = send(tg.at[1], rc, sibling)
    arrived(*l_y2)
    l_far = [
        send(ly.at[2], ly.at[4], along_y(2)),
        send(ly.at[2], ly.at[3], along_y(1)),
        send(ly.at[6], ly.at[5], along_y(-1)),
    ]
    text_part(0)
    arrived(r_core)
    for e in (1, 2, 0):
        tg[0, e] += rc[e]
        if e:
            rz_copy = send(tg.at[0, e], rz.at[e - 1], along_z(-STEP[e]))
            r_z = [rz_copy] if e == 1 else r_z + [rz_copy]

    a_late = y_second(lambda o: xga.at[o], lambda o: rya.at[o], a_far)
    arrived(*l_y1, *l_far)
    lx[0] = jnp.sum(ly[...], axis=0)
    l_x = [send(lx.at[0], lx.at[by % NX], along_x(by)) for by in (2, 1, -1)]

    arrived(*r_z)
    tg[0, 0] += rz[0] + rz[1]
    r_k = [send(tg.at[0, 0, k], rk.at[k - 1], along_z(-3 * k)) for k in (2, 1, 3)]

    arrived(*l_x)
    lz[0, 0] = jnp.sum(lx[...], axis=0)
    l_core = send(lz.at[0, 0], lz.at[0, 1], sibling)

    arrived(*r_x)
    xgb[0] += rxb[0] + rxb[1] + rxb[2]
    b_far, b_near = y_first(lambda o: xgb.at[0, o], lambda o: ryb.at[o])

    arrived(l_core)
    l_z = [send(lz.at[0], lz.at[k], along_z(3 * k)) for k in (2, 1, 3)]

    arrived(*a_late, *a_near)
    xga[0] += (rya[1] + rya[7]) + (rya[2] + rya[6])
    r_a = [send(xga.at[0, ox], rxa.at[ox - 1], along_x(-ox)) for ox in (2, 1, 3)]

    b_late = y_second(lambda o: xgb.at[0, o], lambda o: ryb.at[o], b_far)

    arrived(*r_a)
    image_grad_ref[:, pl.ds(0, CA)] = xga[0, 0] + rxa[0] + rxa[1] + rxa[2]
    arrived(*r_k)
    text_grad_ref[...] = tg[0, 0, 0] + rk[0] + rk[1] + rk[2]

    arrived(*b_near, *b_late)
    image_grad_ref[:, pl.ds(CA, CB)] = xgb[0, 0] + (ryb[1] + ryb[7]) + (ryb[2] + ryb[6])

    arrived(*l_z)
    out = jnp.zeros((8, 128), F32)
    for k in range(4):
        for s in range(2):
            at_txt = lax.div(moved(z, -3 * k, NZ), ZLO) * 2 + (1 - core if s else core)
            for half in range(2):
                picked = jnp.where(lane == own + half, lz[k, s], 0.0)
                value = jnp.sum(picked, axis=1, keepdims=True)
                out = jnp.where(lane == at_txt * ROWS + half * 8 + row, value, out)
    loss_ref[...] = jnp.sum(out, axis=0, keepdims=True)

    for copy in started:
        copy.wait_send()


def per_device(image_emb, text_emb, pairs, log_scale, bias):
    vmem = pl.BlockSpec(memory_space=pltpu.VMEM)
    smem = pl.BlockSpec(memory_space=pltpu.SMEM)
    hbm = pl.BlockSpec(memory_space=pl.ANY)
    images = NX * NY * ROWS
    loss, image_grad, text_grad = pl.pallas_call(
        kernel,
        out_shape=(
            jax.ShapeDtypeStruct((1, 128), F32),
            jax.ShapeDtypeStruct((ROWS, WIDTH), F32),
            jax.ShapeDtypeStruct((ROWS, WIDTH), F32),
        ),
        in_specs=[smem, smem, vmem, hbm, hbm],
        out_specs=(vmem, vmem, vmem),
        scratch_shapes=[
            pltpu.VMEM((NY, NX, ROWS, CA), F32),
            pltpu.VMEM((NX, NY, ROWS, CB), F32),
            pltpu.VMEM((2, 3, 4, ROWS, WIDTH), F32),
            pltpu.VMEM((images, WIDTH), BF16),
            pltpu.VMEM((images, WIDTH), BF16),
            pltpu.VMEM((TEXTS, WIDTH), BF16),
            pltpu.VMEM((TEXTS, WIDTH), BF16),
            pltpu.VMEM((images, TEXTS), BF16),
            pltpu.VMEM((images, TEXTS), BF16),
            pltpu.VMEM((images, 128), F32),
            pltpu.VMEM((NY, NX, ROWS, CA), F32),
            pltpu.VMEM((NX, NY, ROWS, CB), F32),
            pltpu.VMEM((2, 3, 4, ROWS, WIDTH), F32),
            pltpu.VMEM((3, NY, ROWS, CB), F32),
            pltpu.VMEM((NY, NX, ROWS, CA), F32),
            pltpu.VMEM((NY, ROWS, CB), F32),
            pltpu.VMEM((3, ROWS, CA), F32),
            pltpu.VMEM((3, 4, ROWS, WIDTH), F32),
            pltpu.VMEM((2, 4, ROWS, WIDTH), F32),
            pltpu.VMEM((3, ROWS, WIDTH), F32),
            pltpu.VMEM((NY, 8, 128), F32),
            pltpu.VMEM((NX, 8, 128), F32),
            pltpu.VMEM((NY, 8, 128), F32),
            pltpu.VMEM((NX, 8, 128), F32),
            pltpu.VMEM((4, 2, 8, 128), F32),
            pltpu.SemaphoreType.DMA((3,)),
            pltpu.SemaphoreType.DMA((COPIES,)),
            pltpu.SemaphoreType.DMA((COPIES,)),
        ],
        compiler_params=pltpu.CompilerParams(
            collective_id=0, has_side_effects=True, vmem_limit_bytes=40 * 2**20
        ),
        name="contrastive",
    )(log_scale, bias, pairs.reshape(1, 128), image_emb, text_emb)
    return loss.reshape(128), image_grad, text_grad


def solution(mesh):
    return jax.shard_map(
        per_device,
        mesh=mesh,
        in_specs=(P(("img", "txt"), None), P(("txt", "img"), None), P("img"), P(), P()),
        out_specs=(P("img"), P(("img", "txt"), None), P(("txt", "img"), None)),
        check_vma=False,
    )
```

```python
import functools

import jax
import jax.numpy as jnp
from jax import lax
from jax.experimental import pallas as pl
from jax.experimental.pallas import tpu as pltpu
from jax.sharding import PartitionSpec as P

MESH = pl.DeviceIdType.MESH
NX, NY, NZ, ZLO = 4, 8, 12, 3
ROWS, WIDTH = 16, 768
CA = 256
CB = WIDTH - CA
TEXTS = 2 * NZ * ROWS
F32, BF16 = jnp.float32, jnp.bfloat16
COPIES = 128
STEP = (0, 1, -1)
RELAYS = (
    ((0, 1), (0, 2), 3),
    ((0, 1), (2, 2), 2),
    ((0, 3), (1, 2), -2),
    ((0, 1), (1, 1), 1),
    ((0, 1), (2, 1), -1),
    ((0, 3), (2, 3), -1),
    ((0, 3), (1, 3), 1),
)
BLOCK = NX * 4 * ROWS
NEAR, FAR = 0, 1


def at_y(by):
    return (by + 1) % NY


def halves(value):
    high = value.astype(BF16)
    return high, (value - high.astype(F32)).astype(BF16)


def dot3(ah, al, bh, bl, dims):
    def dot(a, b):
        return lax.dot_general(a, b, (dims, ((), ())), preferred_element_type=F32)

    return dot(ah, bh) + (dot(ah, bl) + dot(al, bh))


def kernel(
    log_scale_ref, bias_ref, pairs_ref, image_ref, text_ref,
    loss_ref, image_grad_ref, text_grad_ref,
    ga, gb, tx, xh, xl, th, tl, dh, dl, pc,
    xga, xgb, tg, rxb, rya, ryb, rxa, rc, rz, rk, py, px, ly, lx, lz,
    local_sem, send_sem, recv_sem,
):
    img, txt = lax.axis_index("img"), lax.axis_index("txt")
    column = lax.div(img, ZLO)
    x, y = lax.div(column, NY), lax.rem(column, NY)
    core = lax.rem(txt, 2)
    z = lax.div(txt, 2) * ZLO + lax.rem(img, ZLO)
    way = 1 - 2 * core

    def moved(at, by, size):
        return lax.rem(at + way * by + 2 * size, size)

    def device(at_x, at_y, at_z, at_core):
        return (
            (at_x * NY + at_y) * ZLO + lax.rem(at_z, ZLO),
            lax.div(at_z, ZLO) * 2 + at_core,
        )

    def along_x(by):
        return device(moved(x, by, NX), y, z, core)

    def along_y(by):
        return device(x, moved(y, by, NY), z, core)

    def along_z(by):
        return device(x, y, moved(z, by, NZ), core)

    sibling = device(x, y, z, 1 - core)
    peers = [along_z(by) for by in (3, -3, 2, -2)]
    peers += [along_y(by) for by in (2, -2)] + [along_x(2)]
    peers += [along(by) for along in (along_x, along_y, along_z) for by in (1, -1)]
    peers.append(sibling)

    copies = [
        pltpu.make_async_copy(image_ref.at[:, pl.ds(0, CA)], ga.at[at_y(0), 0], local_sem.at[0]),
        pltpu.make_async_copy(image_ref.at[:, pl.ds(CA, CB)], gb.at[0, at_y(0)], local_sem.at[1]),
        pltpu.make_async_copy(text_ref, tx.at[0, 0, 0], local_sem.at[2]),
    ]
    for copy in copies:
        copy.start()

    barrier = pltpu.get_barrier_semaphore()
    for peer in peers:
        pl.semaphore_signal(barrier, inc=1, device_id=peer, device_id_type=MESH)

    lane = lax.broadcasted_iota(jnp.int32, (8, 128), 1)
    row = lax.broadcasted_iota(jnp.int32, (8, 128), 0)
    own = 2 * (x * NY + y)
    pairs_row = jnp.broadcast_to(pairs_ref[...].astype(F32), (8, 128))
    tile = jnp.zeros((8, 128), F32)
    for half in range(2):
        picked = jnp.where(lane == txt * ROWS + half * 8 + row, pairs_row, 0.0)
        tile = jnp.where(lane == own + half, jnp.sum(picked, axis=1, keepdims=True), tile)
    py[1] = tile

    pl.semaphore_wait(barrier, len(peers))
    for copy in copies:
        copy.wait()

    started = []

    def send(source, target, to):
        at = len(started)
        copy = pltpu.make_async_remote_copy(
            src_ref=source,
            dst_ref=target,
            send_sem=send_sem.at[at],
            recv_sem=recv_sem.at[at],
            device_id=to,
            device_id_type=MESH,
        )
        copy.start()
        started.append(copy)
        return copy

    def arrived(*copies):
        for copy in copies:
            copy.wait_recv()

    def pass_on(slot):
        return [
            send(slot(at_y(2)), slot(at_y(4)), along_y(2)),
            send(slot(at_y(2)), slot(at_y(3)), along_y(1)),
            send(slot(at_y(-2)), slot(at_y(-3)), along_y(-1)),
        ]

    def b_along_x(low, count):
        return [
            send(gb.at[0, pl.ds(low, count)], gb.at[by % NX, pl.ds(low, count)], along_x(by))
            for by in (2, 1, -1)
        ]

    def b_along_y(*steps):
        return {by: send(gb.at[0, 1], gb.at[0, at_y(by)], along_y(by)) for by in steps}

    b_x = [None, None]
    b_y = b_along_y(2, -2)
    t_far = [send(tx.at[0, 0, 0], tx.at[0, 0, k], along_z(by)) for k, by in ((1, 3), (3, -3))]
    a_x = [send(ga.at[1, 0], ga.at[1, by % NX], along_x(by)) for by in (2, 1, -1)]
    b_y |= b_along_y(1, -1)
    b_x[NEAR] = b_along_x(1, 1)
    arrived(*a_x)
    arrived(b_y[2], b_y[-2])
    b_far = pass_on(lambda p: gb.at[0, p])
    b_x[NEAR] += b_along_x(3, 1)
    b_x[FAR] = b_along_x(7, 1)
    a_y = {by: send(ga.at[1], ga.at[at_y(by)], along_y(by)) for by in (2, -2)}
    p_y = {by: send(py.at[1], py.at[at_y(by)], along_y(by)) for by in (2, -2, 1, -1)}
    t_near = [send(tx.at[0, 0, 0], tx.at[0, e, 0], along_z(STEP[e])) for e in (1, 2)]
    arrived(b_y[1], b_y[-1])
    b_x[NEAR] += b_along_x(0, 1) + b_along_x(2, 1)
    arrived(*t_far)
    for near, far, by in RELAYS:
        t_near.append(send(tx.at[(0,) + near], tx.at[(0,) + far], along_z(by)))
    t_core = [send(tx.at[0, 0, pl.ds(0, 2)], tx.at[1, 0, pl.ds(0, 2)], sibling)]
    t_core.append(send(tx.at[0, 0, 3], tx.at[1, 0, 3], sibling))
    a_y |= {by: send(ga.at[1], ga.at[at_y(by)], along_y(by)) for by in (1, -1)}
    arrived(p_y[2], p_y[-2])
    p_far = pass_on(lambda p: py.at[p])
    arrived(*b_far)
    b_x[FAR] += b_along_x(4, 3)
    arrived(a_y[2], a_y[-2])
    a_far = pass_on(lambda p: ga.at[p])
    arrived(p_y[1], p_y[-1], *p_far)
    px[0] = jnp.sum(py[...], axis=0)
    p_x = [send(px.at[0], px.at[by % NX], along_x(by)) for by in (2, 1, -1)]

    places = lax.broadcasted_iota(jnp.int32, (8, TEXTS), 1)
    slot = lax.div(places, ROWS)
    ids = places
    for s in range(2):
        for e in range(3):
            for k in range(4):
                at = (s * 3 + e) * 4 + k
                by = 3 * k + STEP[e]
                at_z = moved(z, by if s else -by, NZ)
                at_core = 1 - core if s else core
                owner = lax.div(at_z, ZLO) * 2 + at_core
                base = owner * (NX * NY * ZLO * ROWS) + (column * ZLO + lax.rem(at_z, ZLO)) * ROWS
                ids = jnp.where(slot == at, places + (base - at * ROWS), ids)
    ids = ids.astype(F32)[0:1]

    arrived(*t_near)
    t_core.append(send(tx.at[0, 0, 2], tx.at[1, 0, 2], sibling))
    t_core.append(send(tx.at[0, pl.ds(1, 2)], tx.at[1, pl.ds(1, 2)], sibling))

    arrived(*p_x)
    matched = jnp.sum(px[...], axis=0)
    groups = [
        (block, ox, inner, half)
        for block in (NEAR, FAR)
        for ox in range(NX)
        for inner in range(4)
        for half in range(2)
    ]

    def lane_of(block, ox, inner, half):
        oy = block * 4 + inner - 1
        return 2 * (moved(x, -ox, NX) * NY + moved(y, -oy, NY)) + half

    for at, group in enumerate(groups):
        picked = jnp.where(lane == lane_of(*group), matched, 0.0)
        spread = jnp.broadcast_to(jnp.sum(picked, axis=1, keepdims=True), (8, 128))
        pc[pl.ds(at * 8, 8), :] = spread

    def split_texts(s):
        high, low = halves(tx[s].reshape(NZ * ROWS, WIDTH))
        th[pl.ds(s * NZ * ROWS, NZ * ROWS), :] = high
        tl[pl.ds(s * NZ * ROWS, NZ * ROWS), :] = low

    def split_images(block):
        for ox in range(NX):
            rows = pl.ds(block * BLOCK + ox * 4 * ROWS, 4 * ROWS)
            high, low = halves(ga[pl.ds(block * 4, 4), ox].reshape(4 * ROWS, CA))
            xh[rows, pl.ds(0, CA)] = high
            xl[rows, pl.ds(0, CA)] = low
            high, low = halves(gb[ox, pl.ds(block * 4, 4)].reshape(4 * ROWS, CB))
            xh[rows, pl.ds(CA, CB)] = high
            xl[rows, pl.ds(CA, CB)] = low

    scale = jnp.exp(jnp.full((8, 128), log_scale_ref[0], F32))[0:1, 0:1]
    shift = bias_ref[0]

    def slopes(block, losses):
        rows = pl.ds(block * BLOCK, BLOCK)
        dots = dot3(xh[rows, :], xl[rows, :], th[...], tl[...], ((1,), (1,)))
        logits = scale * dots + shift
        match = jnp.concatenate([pc[rows, :]] * (TEXTS // 128), axis=1) == ids
        signed = jnp.where(match, -logits, logits)
        small = jnp.exp(-jnp.abs(logits))
        loss = jnp.maximum(signed, 0.0) + jnp.log1p(small)
        loss = sum(loss[:, at * 128 : (at + 1) * 128] for at in range(TEXTS // 128))
        loss = jnp.sum(loss, axis=1, keepdims=True)
        for at, group in enumerate(groups[block * 32 : (block + 1) * 32]):
            losses = jnp.where(lane == lane_of(*group), loss[at * 8 : at * 8 + 8], losses)
        part = 1.0 / (1.0 + small)
        chance = jnp.where(signed >= 0.0, part, small * part)
        high, low = halves(scale * jnp.where(match, -chance, chance))
        dh[rows, :] = high
        dl[rows, :] = low
        return losses

    def image_terms(block):
        rows = pl.ds(block * BLOCK, BLOCK)
        grad = dot3(dh[rows, :], dl[rows, :], th[...], tl[...], ((1,), (0,)))
        inner = pl.ds(block * 4, 4)
        for ox in range(NX):
            part = grad[ox * 4 * ROWS : (ox + 1) * 4 * ROWS].reshape(4, ROWS, WIDTH)
            xgb[ox, inner] = part[:, :, CA:]
            xga[inner, ox] = part[:, :, :CA]

    def terms_along_x(block):
        inner = pl.ds(block * 4, 4)
        return [
            send(xgb.at[ox, inner], rxb.at[ox - 1, inner], along_x(-ox)) for ox in (2, 1, 3)
        ]

    def far_terms(source, target):
        return [
            send(source(at_y(4)), target(at_y(4)), along_y(-2)),
            send(source(at_y(3)), target(at_y(3)), along_y(-1)),
            send(source(at_y(-3)), target(at_y(-3)), along_y(1)),
        ]

    def text_terms(low, count):
        cols = pl.ds(low * ROWS, count * ROWS)
        part = dot3(dh[:, cols], dl[:, cols], xh[...], xl[...], ((0,), (0,)))
        part = part.reshape(count, ROWS, WIDTH)
        for i in range(count):
            s, rest = divmod(low + i, 12)
            e, k = divmod(rest, 4)
            tg[s, e, k] = part[i]

    split_texts(0)
    arrived(*t_core)
    split_texts(1)
    arrived(a_y[1], a_y[-1], *b_x[NEAR])
    split_images(NEAR)
    losses = slopes(NEAR, jnp.zeros((8, 128), F32))
    image_terms(NEAR)
    arrived(*a_far, *b_x[FAR])
    split_images(FAR)
    lx[0] = slopes(FAR, losses)
    l_x = [send(lx.at[0], lx.at[by % NX], along_x(by)) for by in (2, 1, -1)]
    image_terms(FAR)
    ra_far = far_terms(lambda p: xga.at[p], lambda p: rya.at[p])
    r_far = terms_along_x(FAR)

    text_terms(8, 16)
    r_core = send(tg.at[1], rc, sibling)
    r_near = terms_along_x(NEAR)
    arrived(*l_x)
    ly[1] = jnp.sum(lx[...], axis=0)
    l_y = {by: send(ly.at[1], ly.at[at_y(by)], along_y(by)) for by in (2, -2, 1, -1)}
    ra_near = [send(xga.at[at_y(by)], rya.at[at_y(by)], along_y(-by)) for by in (1, -1)]
    text_terms(0, 8)
    arrived(r_core)
    tg[0] += rc[...]
    r_z = {}
    for near, far, by in RELAYS:
        r_z.setdefault(near, []).append(send(tg.at[(0,) + far], rz.at[far], along_z(-by)))
    r_last = [send(tg.at[0, e, 0], rz.at[e, 0], along_z(-STEP[e])) for e in (1, 2)]

    arrived(l_y[2], l_y[-2])
    l_far = pass_on(lambda p: ly.at[p])
    arrived(*ra_far)
    xga[3] += rya[4] + rya[5]
    xga[7] += rya[6]
    ra_near += [send(xga.at[3], rya.at[3], along_y(-2)), send(xga.at[7], rya.at[7], along_y(2))]

    arrived(*r_far)
    xgb[0, pl.ds(4, 4)] += rxb[0, pl.ds(4, 4)] + rxb[1, pl.ds(4, 4)] + rxb[2, pl.ds(4, 4)]
    rb_far = far_terms(lambda p: xgb.at[0, p], lambda p: ryb.at[p])

    arrived(l_y[1], l_y[-1], *l_far)
    lz[0, 0] = jnp.sum(ly[...], axis=0)
    l_core = send(lz.at[0, 0], lz.at[0, 1], sibling)
    arrived(l_core)
    l_z = [send(lz.at[0], lz.at[k], along_z(by)) for k, by in ((1, 3), (3, -3))]

    for at, (near, by) in enumerate((((0, 1), 3), ((0, 3), -3))):
        arrived(*r_z[near])
        tg[(0,) + near] += sum(rz[far] for relay, far, _ in RELAYS if relay == near)
        r_last.append(send(tg.at[(0,) + near], rk.at[at], along_z(-by)))

    arrived(*r_near)
    xgb[0, pl.ds(0, 4)] += rxb[0, pl.ds(0, 4)] + rxb[1, pl.ds(0, 4)] + rxb[2, pl.ds(0, 4)]
    arrived(*rb_far)
    xgb[0, 3] += ryb[4] + ryb[5]
    xgb[0, 7] += ryb[6]
    rb = [send(xgb.at[0, at_y(by)], ryb.at[at_y(by)], along_y(-by)) for by in (2, -2, 1, -1)]

    arrived(*l_z)
    l_last = send(lz.at[1], lz.at[2], along_z(3))

    arrived(*ra_near)
    xga[1] += (rya[0] + rya[2]) + (rya[3] + rya[7])
    r_a = [send(xga.at[1, ox], rxa.at[ox - 1], along_x(-ox)) for ox in (2, 1, 3)]

    arrived(*r_a)
    image_grad_ref[:, pl.ds(0, CA)] = xga[1, 0] + rxa[0] + rxa[1] + rxa[2]
    arrived(*r_last)
    text_grad_ref[...] = (tg[0, 0, 0] + rz[1, 0] + rz[2, 0]) + (rk[0] + rk[1])
    arrived(*rb)
    total = xgb[0, 1]
    for by in (1, -1, 2, -2):
        total += ryb[at_y(by)]
    image_grad_ref[:, pl.ds(CA, CB)] = total

    arrived(l_last)
    out = jnp.zeros((8, 128), F32)
    for k in range(4):
        for s in range(2):
            at_txt = lax.div(moved(z, -3 * k, NZ), ZLO) * 2 + (1 - core if s else core)
            for half in range(2):
                picked = jnp.where(lane == own + half, lz[k, s], 0.0)
                value = jnp.sum(picked, axis=1, keepdims=True)
                out = jnp.where(lane == at_txt * ROWS + half * 8 + row, value, out)
    loss_ref[...] = jnp.sum(out, axis=0, keepdims=True)

    for copy in started:
        copy.wait_send()


def per_device(image_emb, text_emb, pairs, log_scale, bias):
    vmem = pl.BlockSpec(memory_space=pltpu.VMEM)
    smem = pl.BlockSpec(memory_space=pltpu.SMEM)
    hbm = pl.BlockSpec(memory_space=pl.ANY)
    images = NX * NY * ROWS
    in_hbm = functools.partial(pltpu.with_memory_space_constraint, memory_space=pltpu.HBM)
    loss, image_grad, text_grad = pl.pallas_call(
        kernel,
        out_shape=(
            jax.ShapeDtypeStruct((1, 128), F32),
            jax.ShapeDtypeStruct((ROWS, WIDTH), F32),
            jax.ShapeDtypeStruct((ROWS, WIDTH), F32),
        ),
        in_specs=[smem, smem, vmem, hbm, hbm],
        out_specs=(vmem, vmem, vmem),
        scratch_shapes=[
            pltpu.VMEM((NY, NX, ROWS, CA), F32),
            pltpu.VMEM((NX, NY, ROWS, CB), F32),
            pltpu.VMEM((2, 3, 4, ROWS, WIDTH), F32),
            pltpu.VMEM((images, WIDTH), BF16),
            pltpu.VMEM((images, WIDTH), BF16),
            pltpu.VMEM((TEXTS, WIDTH), BF16),
            pltpu.VMEM((TEXTS, WIDTH), BF16),
            pltpu.VMEM((images, TEXTS), BF16),
            pltpu.VMEM((images, TEXTS), BF16),
            pltpu.VMEM((images, 128), F32),
            pltpu.VMEM((NY, NX, ROWS, CA), F32),
            pltpu.VMEM((NX, NY, ROWS, CB), F32),
            pltpu.VMEM((2, 3, 4, ROWS, WIDTH), F32),
            pltpu.VMEM((3, NY, ROWS, CB), F32),
            pltpu.VMEM((NY, NX, ROWS, CA), F32),
            pltpu.VMEM((NY, ROWS, CB), F32),
            pltpu.VMEM((3, ROWS, CA), F32),
            pltpu.VMEM((3, 4, ROWS, WIDTH), F32),
            pltpu.VMEM((3, 4, ROWS, WIDTH), F32),
            pltpu.VMEM((2, ROWS, WIDTH), F32),
            pltpu.VMEM((NY, 8, 128), F32),
            pltpu.VMEM((NX, 8, 128), F32),
            pltpu.VMEM((NY, 8, 128), F32),
            pltpu.VMEM((NX, 8, 128), F32),
            pltpu.VMEM((4, 2, 8, 128), F32),
            pltpu.SemaphoreType.DMA((3,)),
            pltpu.SemaphoreType.DMA((COPIES,)),
            pltpu.SemaphoreType.DMA((COPIES,)),
        ],
        compiler_params=pltpu.CompilerParams(
            collective_id=0, has_side_effects=True, vmem_limit_bytes=40 * 2**20
        ),
        name="contrastive",
    )(log_scale, bias, *(in_hbm(part) for part in (pairs.reshape(1, 128), image_emb, text_emb)))
    return loss.reshape(128), image_grad, text_grad


def solution(mesh):
    return jax.shard_map(
        per_device,
        mesh=mesh,
        in_specs=(P(("img", "txt"), None), P(("txt", "img"), None), P("img"), P(), P()),
        out_specs=(P("img"), P(("img", "txt"), None), P(("txt", "img"), None)),
        check_vma=False,
    )
```

```python
import functools

import jax
import jax.numpy as jnp
from jax import lax
from jax.experimental import pallas as pl
from jax.experimental.pallas import tpu as pltpu
from jax.sharding import PartitionSpec as P

MESH = pl.DeviceIdType.MESH
NX, NY, NZ, ZLO = 4, 8, 12, 3
ROWS, WIDTH = 16, 768
CA = 256
CB = WIDTH - CA
TEXTS = 2 * NZ * ROWS
F32, BF16 = jnp.float32, jnp.bfloat16
COPIES = 128
STEP = (0, 1, -1)
RELAYS = (
    ((0, 1), (0, 2), 3),
    ((0, 1), (2, 2), 2),
    ((0, 3), (1, 2), -2),
    ((0, 1), (1, 1), 1),
    ((0, 1), (2, 1), -1),
    ((0, 3), (2, 3), -1),
    ((0, 3), (1, 3), 1),
)
BLOCK = NX * 4 * ROWS
NEAR, FAR = 0, 1


def at_y(by):
    return (by + 1) % NY


def halves(value):
    high = value.astype(BF16)
    return high, (value - high.astype(F32)).astype(BF16)


def dot3(ah, al, bh, bl, dims):
    def dot(a, b):
        return lax.dot_general(a, b, (dims, ((), ())), preferred_element_type=F32)

    return dot(ah, bh) + (dot(ah, bl) + dot(al, bh))


def kernel(
    log_scale_ref, bias_ref, pairs_ref, image_ref, text_ref,
    loss_ref, image_grad_ref, text_grad_ref,
    ga, gb, tx, xh, xl, th, tl, dh, dl, pc,
    xga, xgb, tg, rxb, rya, ryb, rxa, rc, rz, rk, py, px, ly, lx, lz,
    pairs_here, local_sem, send_sem, recv_sem,
):
    img, txt = lax.axis_index("img"), lax.axis_index("txt")
    column = lax.div(img, ZLO)
    x, y = lax.div(column, NY), lax.rem(column, NY)
    core = lax.rem(txt, 2)
    z = lax.div(txt, 2) * ZLO + lax.rem(img, ZLO)
    way = 1 - 2 * core

    def moved(at, by, size):
        return lax.rem(at + way * by + 2 * size, size)

    def device(at_x, at_y, at_z, at_core):
        return (
            (at_x * NY + at_y) * ZLO + lax.rem(at_z, ZLO),
            lax.div(at_z, ZLO) * 2 + at_core,
        )

    def along_x(by):
        return device(moved(x, by, NX), y, z, core)

    def along_y(by):
        return device(x, moved(y, by, NY), z, core)

    def along_z(by):
        return device(x, y, moved(z, by, NZ), core)

    sibling = device(x, y, z, 1 - core)
    peers = [along_z(by) for by in (3, -3, 2, -2)]
    peers += [along_y(by) for by in (2, -2)] + [along_x(2)]
    peers += [along(by) for along in (along_x, along_y, along_z) for by in (1, -1)]
    peers.append(sibling)

    barrier = pltpu.get_barrier_semaphore()
    for peer in peers:
        pl.semaphore_signal(barrier, inc=1, device_id=peer, device_id_type=MESH)

    copies = [
        pltpu.make_async_copy(pairs_ref, pairs_here, local_sem.at[3]),
        pltpu.make_async_copy(image_ref.at[:, pl.ds(0, CA)], ga.at[at_y(0), 0], local_sem.at[0]),
        pltpu.make_async_copy(image_ref.at[:, pl.ds(CA, CB)], gb.at[0, at_y(0)], local_sem.at[1]),
        pltpu.make_async_copy(text_ref, tx.at[0, 0, 0], local_sem.at[2]),
    ]
    for copy in copies:
        copy.start()

    lane = lax.broadcasted_iota(jnp.int32, (8, 128), 1)
    row = lax.broadcasted_iota(jnp.int32, (8, 128), 0)
    own = 2 * (x * NY + y)
    copies[0].wait()
    pairs_row = jnp.broadcast_to(pairs_here[...].astype(F32), (8, 128))
    tile = jnp.zeros((8, 128), F32)
    for half in range(2):
        picked = jnp.where(lane == txt * ROWS + half * 8 + row, pairs_row, 0.0)
        tile = jnp.where(lane == own + half, jnp.sum(picked, axis=1, keepdims=True), tile)
    py[1] = tile

    pl.semaphore_wait(barrier, len(peers))

    started = []

    def send(source, target, to):
        at = len(started)
        copy = pltpu.make_async_remote_copy(
            src_ref=source,
            dst_ref=target,
            send_sem=send_sem.at[at],
            recv_sem=recv_sem.at[at],
            device_id=to,
            device_id_type=MESH,
        )
        copy.start()
        started.append(copy)
        return copy

    def arrived(*copies):
        for copy in copies:
            copy.wait_recv()

    def pass_on(slot):
        return [
            send(slot(at_y(2)), slot(at_y(4)), along_y(2)),
            send(slot(at_y(2)), slot(at_y(3)), along_y(1)),
            send(slot(at_y(-2)), slot(at_y(-3)), along_y(-1)),
        ]

    own_a, own_b = image_ref.at[:, pl.ds(0, CA)], image_ref.at[:, pl.ds(CA, CB)]

    def b_along_x(low, count):
        return [
            send(gb.at[0, pl.ds(low, count)], gb.at[by % NX, pl.ds(low, count)], along_x(by))
            for by in (2, 1, -1)
        ]

    def b_along_y(*steps):
        return {by: send(own_b, gb.at[0, at_y(by)], along_y(by)) for by in steps}

    b_x = [None, None]
    b_y = b_along_y(2, -2)
    t_far = [send(text_ref, tx.at[0, 0, k], along_z(by)) for k, by in ((1, 3), (3, -3))]
    a_x = [send(own_a, ga.at[1, by % NX], along_x(by)) for by in (2, 1, -1)]
    t_near = {(e, 0): send(text_ref, tx.at[0, e, 0], along_z(STEP[e])) for e in (1, 2)}
    b_y |= b_along_y(1, -1)
    for copy in copies[1:]:
        copy.wait()
    b_x[NEAR] = b_along_x(1, 1)
    arrived(*a_x)
    a_y = {by: send(ga.at[1], ga.at[at_y(by)], along_y(by)) for by in (2, -2)}
    arrived(b_y[2], b_y[-2])
    b_far = pass_on(lambda p: gb.at[0, p])
    b_x[NEAR] += b_along_x(3, 1)
    b_x[FAR] = b_along_x(7, 1)
    p_y = {by: send(py.at[1], py.at[at_y(by)], along_y(by)) for by in (2, -2, 1, -1)}
    arrived(b_y[1], b_y[-1])
    b_x[NEAR] += b_along_x(0, 1) + b_along_x(2, 1)
    arrived(*t_far)
    for near, far, by in RELAYS:
        t_near[far] = send(tx.at[(0,) + near], tx.at[(0,) + far], along_z(by))
    t_core = [send(tx.at[0, 0, pl.ds(0, 2)], tx.at[1, 0, pl.ds(0, 2)], sibling)]
    t_core.append(send(tx.at[0, 0, 3], tx.at[1, 0, 3], sibling))
    a_y |= {by: send(ga.at[1], ga.at[at_y(by)], along_y(by)) for by in (1, -1)}
    arrived(p_y[2], p_y[-2])
    p_far = pass_on(lambda p: py.at[p])
    arrived(*b_far)
    b_x[FAR] += b_along_x(4, 3)
    arrived(a_y[2], a_y[-2])
    a_far = pass_on(lambda p: ga.at[p])
    arrived(p_y[1], p_y[-1], *p_far)
    px[0] = jnp.sum(py[...], axis=0)
    p_x = [send(px.at[0], px.at[by % NX], along_x(by)) for by in (2, 1, -1)]

    places = lax.broadcasted_iota(jnp.int32, (8, TEXTS), 1)
    slot = lax.div(places, ROWS)
    ids = places
    for s in range(2):
        for e in range(3):
            for k in range(4):
                at = (s * 3 + e) * 4 + k
                by = 3 * k + STEP[e]
                at_z = moved(z, by if s else -by, NZ)
                at_core = 1 - core if s else core
                owner = lax.div(at_z, ZLO) * 2 + at_core
                base = owner * (NX * NY * ZLO * ROWS) + (column * ZLO + lax.rem(at_z, ZLO)) * ROWS
                ids = jnp.where(slot == at, places + (base - at * ROWS), ids)
    ids = ids.astype(F32)[0:1]

    for far in ((1, 0), (2, 0), (1, 1), (2, 1), (2, 3), (1, 3), (2, 2), (1, 2), (0, 2)):
        arrived(t_near[far])
        t_core.append(send(tx.at[(0,) + far], tx.at[(1,) + far], sibling))

    arrived(*p_x)
    matched = jnp.sum(px[...], axis=0)
    groups = [
        (block, ox, inner, half)
        for block in (NEAR, FAR)
        for ox in range(NX)
        for inner in range(4)
        for half in range(2)
    ]

    def lane_of(block, ox, inner, half):
        oy = block * 4 + inner - 1
        return 2 * (moved(x, -ox, NX) * NY + moved(y, -oy, NY)) + half

    for at, group in enumerate(groups):
        picked = jnp.where(lane == lane_of(*group), matched, 0.0)
        spread = jnp.broadcast_to(jnp.sum(picked, axis=1, keepdims=True), (8, 128))
        pc[pl.ds(at * 8, 8), :] = spread

    def split_texts(s):
        high, low = halves(tx[s].reshape(NZ * ROWS, WIDTH))
        th[pl.ds(s * NZ * ROWS, NZ * ROWS), :] = high
        tl[pl.ds(s * NZ * ROWS, NZ * ROWS), :] = low

    def split_images(block):
        for ox in range(NX):
            rows = pl.ds(block * BLOCK + ox * 4 * ROWS, 4 * ROWS)
            high, low = halves(ga[pl.ds(block * 4, 4), ox].reshape(4 * ROWS, CA))
            xh[rows, pl.ds(0, CA)] = high
            xl[rows, pl.ds(0, CA)] = low
            high, low = halves(gb[ox, pl.ds(block * 4, 4)].reshape(4 * ROWS, CB))
            xh[rows, pl.ds(CA, CB)] = high
            xl[rows, pl.ds(CA, CB)] = low

    scale = jnp.exp(jnp.full((8, 128), log_scale_ref[0], F32))[0:1, 0:1]
    shift = bias_ref[0]

    def slopes(block, losses):
        rows = pl.ds(block * BLOCK, BLOCK)
        dots = dot3(xh[rows, :], xl[rows, :], th[...], tl[...], ((1,), (1,)))
        logits = scale * dots + shift
        match = jnp.concatenate([pc[rows, :]] * (TEXTS // 128), axis=1) == ids
        signed = jnp.where(match, -logits, logits)
        small = jnp.exp(-jnp.abs(logits))
        loss = jnp.maximum(signed, 0.0) + jnp.log1p(small)
        loss = sum(loss[:, at * 128 : (at + 1) * 128] for at in range(TEXTS // 128))
        loss = jnp.sum(loss, axis=1, keepdims=True)
        for at, group in enumerate(groups[block * 32 : (block + 1) * 32]):
            losses = jnp.where(lane == lane_of(*group), loss[at * 8 : at * 8 + 8], losses)
        part = 1.0 / (1.0 + small)
        chance = jnp.where(signed >= 0.0, part, small * part)
        high, low = halves(scale * jnp.where(match, -chance, chance))
        dh[rows, :] = high
        dl[rows, :] = low
        return losses

    def image_terms(block):
        rows = pl.ds(block * BLOCK, BLOCK)
        grad = dot3(dh[rows, :], dl[rows, :], th[...], tl[...], ((1,), (0,)))
        inner = pl.ds(block * 4, 4)
        for ox in range(NX):
            part = grad[ox * 4 * ROWS : (ox + 1) * 4 * ROWS].reshape(4, ROWS, WIDTH)
            xgb[ox, inner] = part[:, :, CA:]
            xga[inner, ox] = part[:, :, :CA]

    def terms_along_x(block):
        inner = pl.ds(block * 4, 4)
        return [
            send(xgb.at[ox, inner], rxb.at[ox - 1, inner], along_x(-ox)) for ox in (2, 1, 3)
        ]

    def far_terms(source, target):
        return [
            send(source(at_y(4)), target(at_y(4)), along_y(-2)),
            send(source(at_y(3)), target(at_y(3)), along_y(-1)),
            send(source(at_y(-3)), target(at_y(-3)), along_y(1)),
        ]

    def text_terms(low, count):
        cols = pl.ds(low * ROWS, count * ROWS)
        part = dot3(dh[:, cols], dl[:, cols], xh[...], xl[...], ((0,), (0,)))
        part = part.reshape(count, ROWS, WIDTH)
        for i in range(count):
            s, rest = divmod(low + i, 12)
            e, k = divmod(rest, 4)
            tg[s, e, k] = part[i]

    split_texts(0)
    arrived(*t_core)
    split_texts(1)
    arrived(a_y[1], a_y[-1], *b_x[NEAR])
    split_images(NEAR)
    losses = slopes(NEAR, jnp.zeros((8, 128), F32))
    image_terms(NEAR)
    arrived(*a_far, *b_x[FAR])
    split_images(FAR)
    lx[0] = slopes(FAR, losses)
    l_x = [send(lx.at[0], lx.at[by % NX], along_x(by)) for by in (2, 1, -1)]
    image_terms(FAR)
    ra_far = far_terms(lambda p: xga.at[p], lambda p: rya.at[p])
    r_far = terms_along_x(FAR)

    text_terms(8, 16)
    r_core = send(tg.at[1], rc, sibling)
    r_near = terms_along_x(NEAR)
    arrived(*l_x)
    ly[1] = jnp.sum(lx[...], axis=0)
    l_y = {by: send(ly.at[1], ly.at[at_y(by)], along_y(by)) for by in (2, -2, 1, -1)}
    ra_near = [send(xga.at[at_y(by)], rya.at[at_y(by)], along_y(-by)) for by in (1, -1)]
    text_terms(0, 8)
    arrived(r_core)
    tg[0] += rc[...]
    r_z = {}
    for near, far, by in RELAYS:
        r_z.setdefault(near, []).append(send(tg.at[(0,) + far], rz.at[far], along_z(-by)))
    r_last = [send(tg.at[0, e, 0], rz.at[e, 0], along_z(-STEP[e])) for e in (1, 2)]

    arrived(l_y[2], l_y[-2])
    l_far = pass_on(lambda p: ly.at[p])
    arrived(*ra_far)
    xga[3] += rya[4] + rya[5]
    xga[7] += rya[6]
    ra_near += [send(xga.at[3], rya.at[3], along_y(-2)), send(xga.at[7], rya.at[7], along_y(2))]

    arrived(*r_far)
    xgb[0, pl.ds(4, 4)] += rxb[0, pl.ds(4, 4)] + rxb[1, pl.ds(4, 4)] + rxb[2, pl.ds(4, 4)]
    rb_far = far_terms(lambda p: xgb.at[0, p], lambda p: ryb.at[p])

    arrived(l_y[1], l_y[-1], *l_far)
    lz[0, 0] = jnp.sum(ly[...], axis=0)
    l_core = send(lz.at[0, 0], lz.at[0, 1], sibling)
    arrived(l_core)
    l_z = [send(lz.at[0], lz.at[k], along_z(by)) for k, by in ((1, 3), (3, -3))]

    for at, (near, by) in enumerate((((0, 1), 3), ((0, 3), -3))):
        arrived(*r_z[near])
        tg[(0,) + near] += sum(rz[far] for relay, far, _ in RELAYS if relay == near)
        r_last.append(send(tg.at[(0,) + near], rk.at[at], along_z(-by)))

    arrived(*r_near)
    xgb[0, pl.ds(0, 4)] += rxb[0, pl.ds(0, 4)] + rxb[1, pl.ds(0, 4)] + rxb[2, pl.ds(0, 4)]
    arrived(*rb_far)
    xgb[0, 3] += ryb[4] + ryb[5]
    xgb[0, 7] += ryb[6]
    rb = [send(xgb.at[0, at_y(by)], ryb.at[at_y(by)], along_y(-by)) for by in (2, -2, 1, -1)]

    arrived(*l_z)
    l_last = send(lz.at[1], lz.at[2], along_z(3))

    arrived(*ra_near)
    xga[1] += (rya[0] + rya[2]) + (rya[3] + rya[7])
    r_a = [send(xga.at[1, ox], rxa.at[ox - 1], along_x(-ox)) for ox in (2, 1, 3)]

    arrived(*r_a)
    image_grad_ref[:, pl.ds(0, CA)] = xga[1, 0] + rxa[0] + rxa[1] + rxa[2]
    arrived(*r_last)
    text_grad_ref[...] = (tg[0, 0, 0] + rz[1, 0] + rz[2, 0]) + (rk[0] + rk[1])
    arrived(*rb)
    total = xgb[0, 1]
    for by in (1, -1, 2, -2):
        total += ryb[at_y(by)]
    image_grad_ref[:, pl.ds(CA, CB)] = total

    arrived(l_last)
    out = jnp.zeros((8, 128), F32)
    for k in range(4):
        for s in range(2):
            at_txt = lax.div(moved(z, -3 * k, NZ), ZLO) * 2 + (1 - core if s else core)
            for half in range(2):
                picked = jnp.where(lane == own + half, lz[k, s], 0.0)
                value = jnp.sum(picked, axis=1, keepdims=True)
                out = jnp.where(lane == at_txt * ROWS + half * 8 + row, value, out)
    loss_ref[...] = jnp.sum(out, axis=0, keepdims=True)

    for copy in started:
        copy.wait_send()


def per_device(image_emb, text_emb, pairs, log_scale, bias):
    vmem = pl.BlockSpec(memory_space=pltpu.VMEM)
    smem = pl.BlockSpec(memory_space=pltpu.SMEM)
    hbm = pl.BlockSpec(memory_space=pl.ANY)
    images = NX * NY * ROWS
    in_hbm = functools.partial(pltpu.with_memory_space_constraint, memory_space=pltpu.HBM)
    loss, image_grad, text_grad = pl.pallas_call(
        kernel,
        out_shape=(
            jax.ShapeDtypeStruct((1, 128), F32),
            jax.ShapeDtypeStruct((ROWS, WIDTH), F32),
            jax.ShapeDtypeStruct((ROWS, WIDTH), F32),
        ),
        in_specs=[smem, smem, hbm, hbm, hbm],
        out_specs=(vmem, vmem, vmem),
        scratch_shapes=[
            pltpu.VMEM((NY, NX, ROWS, CA), F32),
            pltpu.VMEM((NX, NY, ROWS, CB), F32),
            pltpu.VMEM((2, 3, 4, ROWS, WIDTH), F32),
            pltpu.VMEM((images, WIDTH), BF16),
            pltpu.VMEM((images, WIDTH), BF16),
            pltpu.VMEM((TEXTS, WIDTH), BF16),
            pltpu.VMEM((TEXTS, WIDTH), BF16),
            pltpu.VMEM((images, TEXTS), BF16),
            pltpu.VMEM((images, TEXTS), BF16),
            pltpu.VMEM((images, 128), F32),
            pltpu.VMEM((NY, NX, ROWS, CA), F32),
            pltpu.VMEM((NX, NY, ROWS, CB), F32),
            pltpu.VMEM((2, 3, 4, ROWS, WIDTH), F32),
            pltpu.VMEM((3, NY, ROWS, CB), F32),
            pltpu.VMEM((NY, NX, ROWS, CA), F32),
            pltpu.VMEM((NY, ROWS, CB), F32),
            pltpu.VMEM((3, ROWS, CA), F32),
            pltpu.VMEM((3, 4, ROWS, WIDTH), F32),
            pltpu.VMEM((3, 4, ROWS, WIDTH), F32),
            pltpu.VMEM((2, ROWS, WIDTH), F32),
            pltpu.VMEM((NY, 8, 128), F32),
            pltpu.VMEM((NX, 8, 128), F32),
            pltpu.VMEM((NY, 8, 128), F32),
            pltpu.VMEM((NX, 8, 128), F32),
            pltpu.VMEM((4, 2, 8, 128), F32),
            pltpu.VMEM((1, 128), jnp.int32),
            pltpu.SemaphoreType.DMA((4,)),
            pltpu.SemaphoreType.DMA((COPIES,)),
            pltpu.SemaphoreType.DMA((COPIES,)),
        ],
        compiler_params=pltpu.CompilerParams(
            collective_id=0, has_side_effects=True, vmem_limit_bytes=40 * 2**20
        ),
        name="contrastive",
    )(log_scale, bias, *(in_hbm(part) for part in (pairs.reshape(1, 128), image_emb, text_emb)))
    return loss.reshape(128), image_grad, text_grad


def solution(mesh):
    return jax.shard_map(
        per_device,
        mesh=mesh,
        in_specs=(P(("img", "txt"), None), P(("txt", "img"), None), P("img"), P(), P()),
        out_specs=(P("img"), P(("img", "txt"), None), P(("txt", "img"), None)),
        check_vma=False,
    )
```

```python
import functools

import jax
import jax.numpy as jnp
from jax import lax
from jax.experimental import pallas as pl
from jax.experimental.pallas import tpu as pltpu
from jax.sharding import PartitionSpec as P

MESH = pl.DeviceIdType.MESH
NX, NY, NZ, ZLO = 4, 8, 12, 3
ROWS, WIDTH = 16, 768
CA = 256
CB = WIDTH - CA
TEXTS = 2 * NZ * ROWS
F32, BF16 = jnp.float32, jnp.bfloat16
COPIES = 128
STEP = (0, 1, -1)
RELAYS = (
    ((0, 1), (0, 2), 3),
    ((0, 1), (2, 2), 2),
    ((0, 3), (1, 2), -2),
    ((0, 1), (1, 1), 1),
    ((0, 1), (2, 1), -1),
    ((0, 3), (2, 3), -1),
    ((0, 3), (1, 3), 1),
)
BLOCK = NX * 4 * ROWS
NEAR, FAR = 0, 1


def at_y(by):
    return (by + 1) % NY


def halves(value):
    high = value.astype(BF16)
    return high, (value - high.astype(F32)).astype(BF16)


def dot3(ah, al, bh, bl, dims):
    def dot(a, b):
        return lax.dot_general(a, b, (dims, ((), ())), preferred_element_type=F32)

    return dot(ah, bh) + (dot(ah, bl) + dot(al, bh))


def kernel(
    log_scale_ref, bias_ref, pairs_ref, image_ref, text_ref,
    loss_ref, image_grad_ref, text_grad_ref,
    ga, gb, tx, xh, xl, th, tl, dh, dl, pc,
    xga, xgb, tg, rxb, rya, ryb, rxa, rc, rz, rk, py, px, ly, lx, lz,
    pairs_here, local_sem, send_sem, recv_sem,
):
    img, txt = lax.axis_index("img"), lax.axis_index("txt")
    column = lax.div(img, ZLO)
    x, y = lax.div(column, NY), lax.rem(column, NY)
    core = lax.rem(txt, 2)
    z = lax.div(txt, 2) * ZLO + lax.rem(img, ZLO)
    way = 1 - 2 * core

    def moved(at, by, size):
        return lax.rem(at + way * by + 2 * size, size)

    def device(at_x, at_y, at_z, at_core):
        return (
            (at_x * NY + at_y) * ZLO + lax.rem(at_z, ZLO),
            lax.div(at_z, ZLO) * 2 + at_core,
        )

    def along_x(by):
        return device(moved(x, by, NX), y, z, core)

    def along_y(by):
        return device(x, moved(y, by, NY), z, core)

    def along_z(by):
        return device(x, y, moved(z, by, NZ), core)

    sibling = device(x, y, z, 1 - core)
    peers = [along_z(by) for by in (3, -3, 2, -2)]
    peers += [along_y(by) for by in (2, -2)] + [along_x(2)]
    peers += [along(by) for along in (along_x, along_y, along_z) for by in (1, -1)]
    peers.append(sibling)

    barrier = pltpu.get_barrier_semaphore()
    for peer in peers:
        pl.semaphore_signal(barrier, inc=1, device_id=peer, device_id_type=MESH)

    copies = [
        pltpu.make_async_copy(pairs_ref, pairs_here, local_sem.at[3]),
        pltpu.make_async_copy(image_ref.at[:, pl.ds(0, CA)], ga.at[at_y(0), 0], local_sem.at[0]),
        pltpu.make_async_copy(image_ref.at[:, pl.ds(CA, CB)], gb.at[0, at_y(0)], local_sem.at[1]),
        pltpu.make_async_copy(text_ref, tx.at[0, 0, 0], local_sem.at[2]),
    ]
    for copy in copies:
        copy.start()

    lane = lax.broadcasted_iota(jnp.int32, (8, 128), 1)
    row = lax.broadcasted_iota(jnp.int32, (8, 128), 0)
    own = 2 * (x * NY + y)
    copies[0].wait()
    pairs_row = jnp.broadcast_to(pairs_here[...].astype(F32), (8, 128))
    tile = jnp.zeros((8, 128), F32)
    for half in range(2):
        picked = jnp.where(lane == txt * ROWS + half * 8 + row, pairs_row, 0.0)
        tile = jnp.where(lane == own + half, jnp.sum(picked, axis=1, keepdims=True), tile)
    py[1] = tile

    pl.semaphore_wait(barrier, len(peers))

    started = []

    def send(source, target, to):
        at = len(started)
        copy = pltpu.make_async_remote_copy(
            src_ref=source,
            dst_ref=target,
            send_sem=send_sem.at[at],
            recv_sem=recv_sem.at[at],
            device_id=to,
            device_id_type=MESH,
        )
        copy.start()
        started.append(copy)
        return copy

    def arrived(*copies):
        for copy in copies:
            copy.wait_recv()

    def pass_on(slot):
        return [
            send(slot(at_y(2)), slot(at_y(4)), along_y(2)),
            send(slot(at_y(2)), slot(at_y(3)), along_y(1)),
            send(slot(at_y(-2)), slot(at_y(-3)), along_y(-1)),
        ]

    own_a, own_b = image_ref.at[:, pl.ds(0, CA)], image_ref.at[:, pl.ds(CA, CB)]

    def b_along_x(low, count):
        return [
            send(gb.at[0, pl.ds(low, count)], gb.at[by % NX, pl.ds(low, count)], along_x(by))
            for by in (2, 1, -1)
        ]

    def b_along_y(*steps):
        return {by: send(own_b, gb.at[0, at_y(by)], along_y(by)) for by in steps}

    b_x = [None, None]
    b_y = b_along_y(2, -2)
    t_far = [send(text_ref, tx.at[0, 0, k], along_z(by)) for k, by in ((1, 3), (3, -3))]
    a_x = [send(own_a, ga.at[1, by % NX], along_x(by)) for by in (2, 1, -1)]
    t_near = {(e, 0): send(text_ref, tx.at[0, e, 0], along_z(STEP[e])) for e in (1, 2)}
    b_y |= b_along_y(1, -1)
    for copy in copies[1:]:
        copy.wait()
    b_x[NEAR] = b_along_x(1, 1)
    arrived(*a_x)
    a_y = {by: send(ga.at[1], ga.at[at_y(by)], along_y(by)) for by in (2, -2)}
    arrived(b_y[2], b_y[-2])
    b_far = pass_on(lambda p: gb.at[0, p])
    b_x[NEAR] += b_along_x(3, 1)
    b_x[FAR] = b_along_x(7, 1)
    p_y = {by: send(py.at[1], py.at[at_y(by)], along_y(by)) for by in (2, -2, 1, -1)}
    arrived(b_y[1], b_y[-1])
    b_x[NEAR] += b_along_x(0, 1) + b_along_x(2, 1)
    arrived(*t_far)
    for near, far, by in RELAYS:
        t_near[far] = send(tx.at[(0,) + near], tx.at[(0,) + far], along_z(by))
    t_core = [send(tx.at[0, 0, pl.ds(0, 2)], tx.at[1, 0, pl.ds(0, 2)], sibling)]
    t_core.append(send(tx.at[0, 0, 3], tx.at[1, 0, 3], sibling))
    a_y |= {by: send(ga.at[1], ga.at[at_y(by)], along_y(by)) for by in (1, -1)}
    arrived(p_y[2], p_y[-2])
    p_far = pass_on(lambda p: py.at[p])
    arrived(*b_far)
    b_x[FAR] += b_along_x(4, 3)
    arrived(a_y[2], a_y[-2])
    a_far = pass_on(lambda p: ga.at[p])
    arrived(p_y[1], p_y[-1], *p_far)
    px[0] = jnp.sum(py[...], axis=0)
    p_x = [send(px.at[0], px.at[by % NX], along_x(by)) for by in (2, 1, -1)]

    places = lax.broadcasted_iota(jnp.int32, (8, TEXTS), 1)
    slot = lax.div(places, ROWS)
    ids = places
    for s in range(2):
        for e in range(3):
            for k in range(4):
                at = (s * 3 + e) * 4 + k
                by = 3 * k + STEP[e]
                at_z = moved(z, by if s else -by, NZ)
                at_core = 1 - core if s else core
                owner = lax.div(at_z, ZLO) * 2 + at_core
                base = owner * (NX * NY * ZLO * ROWS) + (column * ZLO + lax.rem(at_z, ZLO)) * ROWS
                ids = jnp.where(slot == at, places + (base - at * ROWS), ids)
    ids = ids.astype(F32)[0:1]

    for far in ((1, 0), (2, 0), (1, 1), (2, 1), (2, 3), (1, 3), (2, 2), (1, 2), (0, 2)):
        arrived(t_near[far])
        t_core.append(send(tx.at[(0,) + far], tx.at[(1,) + far], sibling))

    arrived(*p_x)
    matched = jnp.sum(px[...], axis=0)
    groups = [
        (block, ox, inner, half)
        for block in (NEAR, FAR)
        for ox in range(NX)
        for inner in range(4)
        for half in range(2)
    ]

    def lane_of(block, ox, inner, half):
        oy = block * 4 + inner - 1
        return 2 * (moved(x, -ox, NX) * NY + moved(y, -oy, NY)) + half

    for at, group in enumerate(groups):
        picked = jnp.where(lane == lane_of(*group), matched, 0.0)
        spread = jnp.broadcast_to(jnp.sum(picked, axis=1, keepdims=True), (8, 128))
        pc[pl.ds(at * 8, 8), :] = spread

    def split_texts(s):
        high, low = halves(tx[s].reshape(NZ * ROWS, WIDTH))
        th[pl.ds(s * NZ * ROWS, NZ * ROWS), :] = high
        tl[pl.ds(s * NZ * ROWS, NZ * ROWS), :] = low

    def split_images(block):
        for ox in range(NX):
            rows = pl.ds(block * BLOCK + ox * 4 * ROWS, 4 * ROWS)
            high, low = halves(ga[pl.ds(block * 4, 4), ox].reshape(4 * ROWS, CA))
            xh[rows, pl.ds(0, CA)] = high
            xl[rows, pl.ds(0, CA)] = low
            high, low = halves(gb[ox, pl.ds(block * 4, 4)].reshape(4 * ROWS, CB))
            xh[rows, pl.ds(CA, CB)] = high
            xl[rows, pl.ds(CA, CB)] = low

    scale = jnp.exp(jnp.full((8, 128), log_scale_ref[0], F32))[0:1, 0:1]
    shift = bias_ref[0]

    def slopes(block, losses):
        rows = pl.ds(block * BLOCK, BLOCK)
        dots = dot3(xh[rows, :], xl[rows, :], th[...], tl[...], ((1,), (1,)))
        logits = scale * dots + shift
        match = jnp.concatenate([pc[rows, :]] * (TEXTS // 128), axis=1) == ids
        signed = jnp.where(match, -logits, logits)
        small = jnp.exp(-jnp.abs(logits))
        loss = jnp.maximum(signed, 0.0) + jnp.log1p(small)
        loss = sum(loss[:, at * 128 : (at + 1) * 128] for at in range(TEXTS // 128))
        loss = jnp.sum(loss, axis=1, keepdims=True)
        for at, group in enumerate(groups[block * 32 : (block + 1) * 32]):
            losses = jnp.where(lane == lane_of(*group), loss[at * 8 : at * 8 + 8], losses)
        part = 1.0 / (1.0 + small)
        chance = jnp.where(signed >= 0.0, part, small * part)
        high, low = halves(scale * jnp.where(match, -chance, chance))
        dh[rows, :] = high
        dl[rows, :] = low
        return losses

    def image_terms(block):
        rows = pl.ds(block * BLOCK, BLOCK)
        grad = dot3(dh[rows, :], dl[rows, :], th[...], tl[...], ((1,), (0,)))
        inner = pl.ds(block * 4, 4)
        for ox in range(NX):
            part = grad[ox * 4 * ROWS : (ox + 1) * 4 * ROWS].reshape(4, ROWS, WIDTH)
            xgb[ox, inner] = part[:, :, CA:]
            xga[inner, ox] = part[:, :, :CA]

    def terms_along_x(block):
        inner = pl.ds(block * 4, 4)
        return [
            send(xgb.at[ox, inner], rxb.at[ox - 1, inner], along_x(-ox)) for ox in (2, 1, 3)
        ]

    def far_terms(source, target):
        return [
            send(source(at_y(4)), target(at_y(4)), along_y(-2)),
            send(source(at_y(3)), target(at_y(3)), along_y(-1)),
            send(source(at_y(-3)), target(at_y(-3)), along_y(1)),
        ]

    def text_terms(low, count):
        cols = pl.ds(low * ROWS, count * ROWS)
        part = dot3(dh[:, cols], dl[:, cols], xh[...], xl[...], ((0,), (0,)))
        part = part.reshape(count, ROWS, WIDTH)
        for i in range(count):
            s, rest = divmod(low + i, 12)
            e, k = divmod(rest, 4)
            tg[s, e, k] = part[i]

    split_texts(0)
    arrived(*t_core)
    split_texts(1)
    arrived(a_y[1], a_y[-1], *b_x[NEAR])
    split_images(NEAR)
    losses = slopes(NEAR, jnp.zeros((8, 128), F32))
    image_terms(NEAR)
    arrived(*a_far, *b_x[FAR])
    split_images(FAR)
    lx[0] = slopes(FAR, losses)
    l_x = [send(lx.at[0], lx.at[by % NX], along_x(by)) for by in (2, 1, -1)]
    image_terms(FAR)
    ra_far = far_terms(lambda p: xga.at[p], lambda p: rya.at[p])
    r_far = terms_along_x(FAR)

    text_terms(8, 16)
    r_core = {e: send(tg.at[1, e], rc.at[e], sibling) for e in (0, 2, 1)}
    r_near = terms_along_x(NEAR)
    arrived(*l_x)
    ly[1] = jnp.sum(lx[...], axis=0)
    l_y = {by: send(ly.at[1], ly.at[at_y(by)], along_y(by)) for by in (2, -2, 1, -1)}
    ra_near = [send(xga.at[at_y(by)], rya.at[at_y(by)], along_y(-by)) for by in (1, -1)]
    text_terms(0, 8)
    r_z = {}
    for e in (0, 2, 1):
        arrived(r_core[e])
        tg[0, e] += rc[e]
        for near, far, by in RELAYS:
            if far[0] == e:
                r_z.setdefault(near, []).append(send(tg.at[(0,) + far], rz.at[far], along_z(-by)))
    r_last = [send(tg.at[0, e, 0], rz.at[e, 0], along_z(-STEP[e])) for e in (1, 2)]

    arrived(l_y[2], l_y[-2])
    l_far = pass_on(lambda p: ly.at[p])
    arrived(*ra_far)
    xga[3] += rya[4] + rya[5]
    xga[7] += rya[6]
    ra_near += [send(xga.at[3], rya.at[3], along_y(-2)), send(xga.at[7], rya.at[7], along_y(2))]

    arrived(*r_far)
    xgb[0, pl.ds(4, 4)] += rxb[0, pl.ds(4, 4)] + rxb[1, pl.ds(4, 4)] + rxb[2, pl.ds(4, 4)]
    rb_far = far_terms(lambda p: xgb.at[0, p], lambda p: ryb.at[p])

    arrived(l_y[1], l_y[-1], *l_far)
    lz[0, 0] = jnp.sum(ly[...], axis=0)
    l_core = send(lz.at[0, 0], lz.at[0, 1], sibling)
    arrived(l_core)
    l_z = [send(lz.at[0], lz.at[k], along_z(by)) for k, by in ((1, 3), (3, -3))]

    for at, (near, by) in enumerate((((0, 1), 3), ((0, 3), -3))):
        arrived(*r_z[near])
        tg[(0,) + near] += sum(rz[far] for relay, far, _ in RELAYS if relay == near)
        r_last.append(send(tg.at[(0,) + near], rk.at[at], along_z(-by)))

    arrived(*r_near)
    xgb[0, pl.ds(0, 4)] += rxb[0, pl.ds(0, 4)] + rxb[1, pl.ds(0, 4)] + rxb[2, pl.ds(0, 4)]
    arrived(*rb_far)
    xgb[0, 3] += ryb[4] + ryb[5]
    xgb[0, 7] += ryb[6]
    rb = [send(xgb.at[0, at_y(by)], ryb.at[at_y(by)], along_y(-by)) for by in (2, -2, 1, -1)]

    arrived(*l_z)
    l_last = send(lz.at[1], lz.at[2], along_z(3))

    arrived(*ra_near)
    xga[1] += (rya[0] + rya[2]) + (rya[3] + rya[7])
    r_a = [send(xga.at[1, ox], rxa.at[ox - 1], along_x(-ox)) for ox in (2, 1, 3)]

    arrived(*r_a)
    image_grad_ref[:, pl.ds(0, CA)] = xga[1, 0] + rxa[0] + rxa[1] + rxa[2]
    arrived(*r_last)
    text_grad_ref[...] = (tg[0, 0, 0] + rz[1, 0] + rz[2, 0]) + (rk[0] + rk[1])
    arrived(*rb)
    total = xgb[0, 1]
    for by in (1, -1, 2, -2):
        total += ryb[at_y(by)]
    image_grad_ref[:, pl.ds(CA, CB)] = total

    arrived(l_last)
    out = jnp.zeros((8, 128), F32)
    for k in range(4):
        for s in range(2):
            at_txt = lax.div(moved(z, -3 * k, NZ), ZLO) * 2 + (1 - core if s else core)
            for half in range(2):
                picked = jnp.where(lane == own + half, lz[k, s], 0.0)
                value = jnp.sum(picked, axis=1, keepdims=True)
                out = jnp.where(lane == at_txt * ROWS + half * 8 + row, value, out)
    loss_ref[...] = jnp.sum(out, axis=0, keepdims=True)

    for copy in started:
        copy.wait_send()


def per_device(image_emb, text_emb, pairs, log_scale, bias):
    vmem = pl.BlockSpec(memory_space=pltpu.VMEM)
    smem = pl.BlockSpec(memory_space=pltpu.SMEM)
    hbm = pl.BlockSpec(memory_space=pl.ANY)
    images = NX * NY * ROWS
    in_hbm = functools.partial(pltpu.with_memory_space_constraint, memory_space=pltpu.HBM)
    loss, image_grad, text_grad = pl.pallas_call(
        kernel,
        out_shape=(
            jax.ShapeDtypeStruct((1, 128), F32),
            jax.ShapeDtypeStruct((ROWS, WIDTH), F32),
            jax.ShapeDtypeStruct((ROWS, WIDTH), F32),
        ),
        in_specs=[smem, smem, hbm, hbm, hbm],
        out_specs=(vmem, vmem, vmem),
        scratch_shapes=[
            pltpu.VMEM((NY, NX, ROWS, CA), F32),
            pltpu.VMEM((NX, NY, ROWS, CB), F32),
            pltpu.VMEM((2, 3, 4, ROWS, WIDTH), F32),
            pltpu.VMEM((images, WIDTH), BF16),
            pltpu.VMEM((images, WIDTH), BF16),
            pltpu.VMEM((TEXTS, WIDTH), BF16),
            pltpu.VMEM((TEXTS, WIDTH), BF16),
            pltpu.VMEM((images, TEXTS), BF16),
            pltpu.VMEM((images, TEXTS), BF16),
            pltpu.VMEM((images, 128), F32),
            pltpu.VMEM((NY, NX, ROWS, CA), F32),
            pltpu.VMEM((NX, NY, ROWS, CB), F32),
            pltpu.VMEM((2, 3, 4, ROWS, WIDTH), F32),
            pltpu.VMEM((3, NY, ROWS, CB), F32),
            pltpu.VMEM((NY, NX, ROWS, CA), F32),
            pltpu.VMEM((NY, ROWS, CB), F32),
            pltpu.VMEM((3, ROWS, CA), F32),
            pltpu.VMEM((3, 4, ROWS, WIDTH), F32),
            pltpu.VMEM((3, 4, ROWS, WIDTH), F32),
            pltpu.VMEM((2, ROWS, WIDTH), F32),
            pltpu.VMEM((NY, 8, 128), F32),
            pltpu.VMEM((NX, 8, 128), F32),
            pltpu.VMEM((NY, 8, 128), F32),
            pltpu.VMEM((NX, 8, 128), F32),
            pltpu.VMEM((4, 2, 8, 128), F32),
            pltpu.VMEM((1, 128), jnp.int32),
            pltpu.SemaphoreType.DMA((4,)),
            pltpu.SemaphoreType.DMA((COPIES,)),
            pltpu.SemaphoreType.DMA((COPIES,)),
        ],
        compiler_params=pltpu.CompilerParams(
            collective_id=0, has_side_effects=True, vmem_limit_bytes=40 * 2**20
        ),
        name="contrastive",
    )(log_scale, bias, *(in_hbm(part) for part in (pairs.reshape(1, 128), image_emb, text_emb)))
    return loss.reshape(128), image_grad, text_grad


def solution(mesh):
    return jax.shard_map(
        per_device,
        mesh=mesh,
        in_specs=(P(("img", "txt"), None), P(("txt", "img"), None), P("img"), P(), P()),
        out_specs=(P("img"), P(("img", "txt"), None), P(("txt", "img"), None)),
        check_vma=False,
    )
```
